32 devices in a mesh: groups: 2 (over x), ctx: 8 (over z, y), dp: 2 (over core).
Axes of the slice: x: 2, y: 2, z: 4, core: 2. Of those that a mesh axis runs over, the one named last changes fastest.
Arguments:
- activations: bfloat16 [2, 8, 2560, 4096], P(None, ('groups', 'dp'), 'ctx'), parts along dimension 1, may hold values from -6 to 6
- out_grads: bfloat16 [2, 8, 2560, 4096], P(None, ('groups', 'dp'), 'ctx'), parts along dimension 1, may hold values from -6 to 6
- input_basis: bfloat16 [2, 4096, 64], replicated, may hold values from -0.09375 to 0.09375
- output_basis: bfloat16 [2, 4096, 64], replicated, may hold values from -0.09375 to 0.09375
- query_grads: float32 [256, 8192], P(('groups', 'ctx', 'dp')), parts along dimension 0, may hold values from -0.0625 to 0.0625
- doc_length: int32 [8], P(('groups', 'dp')), parts along dimension 0, may hold values from 640 to 2560, as said below
- doc_rank: int32 [8], P('groups'), parts along dimension 0, may hold values from 0 to 3, each once
Outputs:
- scores: float32 [8, 128], P(('groups', 'dp')), parts along dimension 0
The draws below stay inside these ranges and needn't reach their ends.
There are 2 independent parts, one for each index of `groups`. The reference program is written for one: setup_inputs(seed, part) draws one part's arguments, and reference() takes and returns one part's arrays. A program takes and returns all parts, laid end to end along the dimension named above; an argument that names none is the same for every part. Nothing has to cross between parts.
Inputs may be any that keep to these rules, and one draw needn't show every extreme that they name: `doc_length`: some document has all 2560 tokens valid in every draw. `doc_rank`: each row number once.
All inputs are finite; a program needn't handle non-finite values.
Results may differ from the reference program's by a relative error of at most 0.0043.
Values sent between devices are 32-bit elements; how exact they have to be, the bound alone decides.
No kernel may reach another device: no remote copies, remote signals or barrier semaphores. Data moves between devices by JAX's collectives and lax.ppermute only.
A program may use at most 128 MiB of HBM per device.

```python
import jax
import jax.numpy as jnp
from jax import lax

D = 4096
R = 64
L = 2
SEG = 2560
DOCS = 4
QUERIES = 128


def draw_doc_length(key, part):
    key = jax.random.fold_in(key, 1)
    first, second = jax.random.split(key)
    counts = jax.random.randint(first, (DOCS,), SEG // 4, SEG + 1)
    chosen = jax.random.randint(second, (), 0, DOCS)
    return jnp.where(jnp.arange(DOCS) == chosen, SEG, counts).astype(jnp.int32)


def block_levels(stream_key, dims, cuts, smallest, largest):
    gain = 1.0
    for dim, shards_of in cuts:
        heights = jax.random.uniform(jax.random.fold_in(jax.random.fold_in(stream_key, 6), dim), (shards_of,), jnp.float32, smallest / len(cuts), largest / len(cuts))
        gain = gain * jnp.repeat(jnp.exp(heights), dims[dim] // shards_of).reshape((-1,) + (1,) * (len(dims) - 1 - dim))
    return gain


def scatter_about(rng, shape, scale, most, pieces=(), held_as=jnp.bfloat16):
    gain = block_levels(rng, shape, pieces, -0.22, 0.18) if pieces else 1.0
    array = jax.random.normal(rng, shape, jnp.float32) * scale * gain
    return jnp.minimum(jnp.maximum(array, -most), most).astype(held_as)


def setup_inputs(seed: int = 0, part: int = 0) -> dict:
    splits = jax.random.split(jax.random.key(seed), 8)
    part_keys = jax.random.split(jax.random.fold_in(splits[7], part), 8)
    return {
        "activations": scatter_about(part_keys[0], (L, DOCS, SEG, D), 1.0, 6.0, ((1, 2), (2, 8))),
        "out_grads": scatter_about(part_keys[1], (L, DOCS, SEG, D), 1.0, 6.0, ((1, 2), (2, 8))),
        "input_basis": scatter_about(splits[2], (L, D, R), D ** -0.5, 0.09375),
        "output_basis": scatter_about(splits[3], (L, D, R), D ** -0.5, 0.09375),
        "query_grads": scatter_about(part_keys[4], (QUERIES, L * R * R), (L * R * R) ** -0.5, 0.0625, ((0, 16),), jnp.float32),
        "doc_length": draw_doc_length(jax.random.fold_in(jax.random.fold_in(splits[7], part), 71), part),
        "doc_rank": jax.random.permutation(part_keys[6], DOCS).astype(jnp.int32),
    }


def reference(activations, out_grads, input_basis, output_basis, query_grads, doc_length, doc_rank):
    valid = (jnp.arange(SEG)[None, :] < doc_length[:, None]).astype(jnp.bfloat16)
    scale = lax.rsqrt(doc_length.astype(jnp.float32))
    layers = []
    for layer in range(L):
        flat_in = activations[layer].reshape(DOCS * SEG, D)
        flat_out = out_grads[layer].reshape(DOCS * SEG, D)
        in_rows = jnp.dot(flat_in, input_basis[layer], preferred_element_type=jnp.float32).astype(jnp.bfloat16)
        out_rows = jnp.dot(flat_out, output_basis[layer], preferred_element_type=jnp.float32).astype(jnp.bfloat16)
        in_rows = in_rows.reshape(DOCS, SEG, R)
        out_rows = out_rows.reshape(DOCS, SEG, R) * valid[:, :, None]
        summed = jnp.einsum('kti,ktj->kij', out_rows.astype(jnp.float32), in_rows.astype(jnp.float32))
        layers.append(summed * scale[:, None, None])
    doc_grad = jnp.stack(layers, axis=1).reshape(DOCS, L * R * R)
    raw = jnp.dot(doc_grad, query_grads.T, precision=lax.Precision.HIGHEST, preferred_element_type=jnp.float32)
    return jnp.zeros((DOCS, QUERIES), jnp.float32).at[doc_rank].set(raw)
```

```python
import functools

import jax
import jax.numpy as jnp
from jax import lax
from jax.experimental import pallas as pl
from jax.experimental.pallas import tpu as pltpu
from jax.sharding import PartitionSpec as P

LANES = 128
BY_LAST = (((1,), (1,)), ((), ()))
BY_FIRST = (((0,), (0,)), ((), ()))


def partial_kernel(
    length_ref, act_ref, outg_ref, inb_ref, outb_ref, query_ref, send_ref,
    act_buf, outg_buf, inb, outb, square, act_sem, outg_sem, basis_sem,
):
    layers, docs, tok, _ = act_ref.shape
    rank = inb_ref.shape[1]
    peers = send_ref.shape[0]
    per_layer = peers // layers
    rows = rank * rank // LANES // per_layer
    many = query_ref.shape[0]
    first = lax.axis_index("ctx") * tok
    pairs = [(layer, doc) for layer in range(layers) for doc in range(docs)]

    def copies(i):
        layer, doc = pairs[i]
        return (
            pltpu.make_async_copy(outg_ref.at[layer, doc], outg_buf.at[i], outg_sem.at[i]),
            pltpu.make_async_copy(act_ref.at[layer, doc], act_buf.at[i], act_sem.at[i]),
        )

    def bases(layer):
        return (
            pltpu.make_async_copy(outb_ref.at[layer], outb.at[layer], basis_sem.at[layer, 0]),
            pltpu.make_async_copy(inb_ref.at[layer], inb.at[layer], basis_sem.at[layer, 1]),
        )

    def has_tokens(doc):
        return first < length_ref[doc]

    for i, (layer, doc) in enumerate(pairs):
        if doc == 0:
            for copy in bases(layer):
                copy.start()

        @pl.when(has_tokens(doc))
        def _(i=i):
            for copy in copies(i):
                copy.start()

    for peer in range(peers):
        for row in range(rows):
            start = (peer * rows + row) * LANES
            at = docs * rows + row * many
            send_ref[peer, at : at + many, :] = query_ref[:, start : start + LANES]

    for i, (layer, doc) in enumerate(pairs):
        if doc == 0:
            for copy in bases(layer):
                copy.wait()

        @pl.when(has_tokens(doc))
        def _(i=i, layer=layer, doc=doc):
            for copy in copies(i):
                copy.wait()
            out_rows = lax.dot_general(
                outg_buf[i], outb[layer], BY_LAST, preferred_element_type=jnp.float32
            )
            in_rows = lax.dot_general(
                act_buf[i], inb[layer], BY_LAST, preferred_element_type=jnp.float32
            )
            position = first + lax.broadcasted_iota(jnp.int32, out_rows.shape, 0)
            out_rows = jnp.where(position < length_ref[doc], out_rows, 0.0).astype(jnp.bfloat16)
            square[...] = lax.dot_general(
                out_rows, in_rows.astype(jnp.bfloat16), BY_FIRST, preferred_element_type=jnp.float32
            )
            scale = lax.rsqrt(jnp.full((1, 1), length_ref[doc], jnp.int32).astype(jnp.float32))
            flat = scale * jnp.concatenate(
                [square[pl.ds(0, rank // 2, stride=2), :], square[pl.ds(1, rank // 2, stride=2), :]],
                axis=1,
            )
            for j in range(per_layer):
                send_ref[layer * per_layer + j, doc * rows : (doc + 1) * rows, :] = flat[
                    j * rows : (j + 1) * rows
                ]

        @pl.when(jnp.logical_not(has_tokens(doc)))
        def _(layer=layer, doc=doc):
            for j in range(per_layer):
                send_ref[layer * per_layer + j, doc * rows : (doc + 1) * rows, :] = jnp.zeros(
                    (rows, LANES), jnp.float32
                )


def score_kernel(docs, rows, many, dp, rank_ref, got_ref, send_ref):
    peers = got_ref.shape[0]
    total = dp * docs
    sums = []
    for d in range(dp):
        part = got_ref[d, : docs * rows, :]
        for c in range(1, peers // dp):
            part = part + got_ref[c * dp + d, : docs * rows, :]
        sums.append(part)
    score = jnp.zeros((total, peers * many), jnp.float32)
    for row in range(rows):
        grad = jnp.concatenate(
            [sums[d][k * rows + row : k * rows + row + 1] for d in range(dp) for k in range(docs)], axis=0
        )
        at = docs * rows + row * many
        query = got_ref[:, at : at + many, :].reshape(peers * many, LANES)
        score = score + lax.dot_general(
            grad, query, BY_LAST, precision=lax.Precision.HIGHEST, preferred_element_type=jnp.float32
        )
    placed = []
    for want in range(total):
        line = jnp.zeros((1, peers * many), jnp.float32)
        for k in range(total):
            line = jnp.where(rank_ref[k] == want, score[k : k + 1], line)
        placed.append(line)
    for d in range(dp):
        mine = jnp.concatenate(placed[d * docs : (d + 1) * docs], axis=0)
        for c in range(peers // dp):
            send_ref[c * dp + d] = mine


def sum_kernel(got_ref, out_ref):
    out_ref[...] = jnp.sum(got_ref[...], axis=0)


def local(mesh_shape, activations, out_grads, input_basis, output_basis, query_grads, doc_length, doc_rank):
    layers, docs, tok, width = activations.shape
    rank = input_basis.shape[2]
    many = query_grads.shape[0]
    dp = mesh_shape["dp"]
    peers = mesh_shape["ctx"] * dp
    rows = layers * rank * rank // LANES // peers
    pairs = layers * docs
    anywhere = pl.BlockSpec(memory_space=pl.ANY)
    vmem = pl.BlockSpec(memory_space=pltpu.VMEM)
    smem = pl.BlockSpec(memory_space=pltpu.SMEM)
    send = pl.pallas_call(
        partial_kernel,
        out_shape=jax.ShapeDtypeStruct((peers, (docs + many) * rows, LANES), jnp.float32),
        in_specs=[smem, anywhere, anywhere, anywhere, anywhere, vmem],
        out_specs=vmem,
        scratch_shapes=[
            pltpu.VMEM((pairs, tok, width), jnp.bfloat16),
            pltpu.VMEM((pairs, tok, width), jnp.bfloat16),
            pltpu.VMEM((layers, rank, width), jnp.bfloat16),
            pltpu.VMEM((layers, rank, width), jnp.bfloat16),
            pltpu.VMEM((rank, rank), jnp.float32),
            pltpu.SemaphoreType.DMA((pairs,)),
            pltpu.SemaphoreType.DMA((pairs,)),
            pltpu.SemaphoreType.DMA((layers, 2)),
        ],
        compiler_params=pltpu.CompilerParams(vmem_limit_bytes=60 << 20),
        name="partial_grads",
    )(
        doc_length,
        activations,
        out_grads,
        jnp.swapaxes(input_basis, 1, 2),
        jnp.swapaxes(output_basis, 1, 2),
        query_grads,
    )
    got = lax.all_to_all(send, ("ctx", "dp"), 0, 0)
    scores = pl.pallas_call(
        functools.partial(score_kernel, docs, rows, many, dp),
        out_shape=jax.ShapeDtypeStruct((peers, docs, peers * many), jnp.float32),
        in_specs=[smem, vmem],
        out_specs=vmem,
        name="column_scores",
    )(doc_rank, got)
    got = lax.all_to_all(scores, ("ctx", "dp"), 0, 0)
    return pl.pallas_call(
        sum_kernel,
        out_shape=jax.ShapeDtypeStruct((docs, peers * many), jnp.float32),
        in_specs=[vmem],
        out_specs=vmem,
        name="sum_scores",
    )(got)


def solution(mesh):
    return jax.shard_map(
        functools.partial(local, dict(mesh.shape)),
        mesh=mesh,
        in_specs=(
            P(None, ("groups", "dp"), "ctx", None),
            P(None, ("groups", "dp"), "ctx", None),
            P(),
            P(),
            P(("groups", "ctx", "dp"), None),
            P(("groups", "dp")),
            P("groups"),
        ),
        out_specs=P(("groups", "dp"), None),
        check_vma=False,
    )
```

```python
import functools

import jax
import jax.numpy as jnp
from jax import lax
from jax.experimental import pallas as pl
from jax.experimental.pallas import tpu as pltpu
from jax.sharding import PartitionSpec as P

LANES = 128
BY_LAST = (((1,), (1,)), ((), ()))
BY_FIRST = (((0,), (0,)), ((), ()))


def partial_kernel(
    length_ref, act_ref, outg_ref, inb_ref, outb_ref, query_ref, send_ref,
    act_buf, outg_buf, inb, outb, square, act_sem, outg_sem, basis_sem,
):
    layers, docs, tok, _ = act_ref.shape
    rank = inb_ref.shape[1]
    peers = send_ref.shape[0]
    per_layer = peers // layers
    rows = rank * rank // LANES // per_layer
    many = query_ref.shape[0]
    first = lax.axis_index("ctx") * tok
    pairs = [(layer, doc) for layer in range(layers) for doc in range(docs)]

    def copies(i):
        layer, doc = pairs[i]
        return (
            pltpu.make_async_copy(outg_ref.at[layer, doc], outg_buf.at[i], outg_sem.at[i]),
            pltpu.make_async_copy(act_ref.at[layer, doc], act_buf.at[i], act_sem.at[i]),
        )

    def bases(layer):
        return (
            pltpu.make_async_copy(outb_ref.at[layer], outb.at[layer], basis_sem.at[layer, 0]),
            pltpu.make_async_copy(inb_ref.at[layer], inb.at[layer], basis_sem.at[layer, 1]),
        )

    def has_tokens(doc):
        return first < length_ref[doc]

    for i, (layer, doc) in enumerate(pairs):
        if doc == 0:
            for copy in bases(layer):
                copy.start()

        @pl.when(has_tokens(doc))
        def _(i=i):
            for copy in copies(i):
                copy.start()

    for peer in range(peers):
        for row in range(rows):
            start = (peer * rows + row) * LANES
            at = docs * rows + row * many
            send_ref[peer, at : at + many, :] = query_ref[:, start : start + LANES]

    for i, (layer, doc) in enumerate(pairs):
        if doc == 0:
            for copy in bases(layer):
                copy.wait()

        @pl.when(has_tokens(doc))
        def _(i=i, layer=layer, doc=doc):
            for copy in copies(i):
                copy.wait()
            out_rows = lax.dot_general(
                outg_buf[i], outb[layer], BY_LAST, preferred_element_type=jnp.float32
            )
            in_rows = lax.dot_general(
                act_buf[i], inb[layer], BY_LAST, preferred_element_type=jnp.float32
            )
            position = first + lax.broadcasted_iota(jnp.int32, out_rows.shape, 0)
            out_rows = jnp.where(position < length_ref[doc], out_rows, 0.0).astype(jnp.bfloat16)
            square[...] = lax.dot_general(
                out_rows, in_rows.astype(jnp.bfloat16), BY_FIRST, preferred_element_type=jnp.float32
            )
            scale = lax.rsqrt(jnp.full((1, 1), length_ref[doc], jnp.int32).astype(jnp.float32))
            flat = scale * jnp.concatenate(
                [square[pl.ds(0, rank // 2, stride=2), :], square[pl.ds(1, rank // 2, stride=2), :]],
                axis=1,
            )
            for j in range(per_layer):
                send_ref[layer * per_layer + j, doc * rows : (doc + 1) * rows, :] = flat[
                    j * rows : (j + 1) * rows
                ]

        @pl.when(jnp.logical_not(has_tokens(doc)))
        def _(layer=layer, doc=doc):
            for j in range(per_layer):
                send_ref[layer * per_layer + j, doc * rows : (doc + 1) * rows, :] = jnp.zeros(
                    (rows, LANES), jnp.float32
                )


def score_kernel(docs, rows, many, dp, rank_ref, got_ref, send_ref):
    peers = got_ref.shape[0]
    total = dp * docs
    sums = []
    for d in range(dp):
        part = got_ref[d, : docs * rows, :]
        for c in range(1, peers // dp):
            part = part + got_ref[c * dp + d, : docs * rows, :]
        sums.append(part)
    score = jnp.zeros((total, peers * many), jnp.float32)
    for row in range(rows):
        grad = jnp.concatenate(
            [sums[d][k * rows + row : k * rows + row + 1] for d in range(dp) for k in range(docs)], axis=0
        )
        at = docs * rows + row * many
        query = got_ref[:, at : at + many, :].reshape(peers * many, LANES)
        score = score + lax.dot_general(
            grad, query, BY_LAST, precision=lax.Precision.HIGHEST, preferred_element_type=jnp.float32
        )
    placed = []
    for want in range(total):
        line = jnp.zeros((1, peers * many), jnp.float32)
        for k in range(total):
            line = jnp.where(rank_ref[k] == want, score[k : k + 1], line)
        placed.append(line)
    for d in range(dp):
        mine = jnp.concatenate(placed[d * docs : (d + 1) * docs], axis=0)
        for c in range(peers // dp):
            send_ref[c * dp + d] = mine


def local(mesh_shape, activations, out_grads, input_basis, output_basis, query_grads, doc_length, doc_rank):
    layers, docs, tok, width = activations.shape
    rank = input_basis.shape[2]
    many = query_grads.shape[0]
    dp = mesh_shape["dp"]
    peers = mesh_shape["ctx"] * dp
    rows = layers * rank * rank // LANES // peers
    pairs = layers * docs
    anywhere = pl.BlockSpec(memory_space=pl.ANY)
    vmem = pl.BlockSpec(memory_space=pltpu.VMEM)
    smem = pl.BlockSpec(memory_space=pltpu.SMEM)
    send = pl.pallas_call(
        partial_kernel,
        out_shape=jax.ShapeDtypeStruct((peers, (docs + many) * rows, LANES), jnp.float32),
        in_specs=[smem, anywhere, anywhere, anywhere, anywhere, vmem],
        out_specs=vmem,
        scratch_shapes=[
            pltpu.VMEM((pairs, tok, width), jnp.bfloat16),
            pltpu.VMEM((pairs, tok, width), jnp.bfloat16),
            pltpu.VMEM((layers, rank, width), jnp.bfloat16),
            pltpu.VMEM((layers, rank, width), jnp.bfloat16),
            pltpu.VMEM((rank, rank), jnp.float32),
            pltpu.SemaphoreType.DMA((pairs,)),
            pltpu.SemaphoreType.DMA((pairs,)),
            pltpu.SemaphoreType.DMA((layers, 2)),
        ],
        compiler_params=pltpu.CompilerParams(vmem_limit_bytes=60 << 20),
        name="partial_grads",
    )(
        doc_length,
        activations,
        out_grads,
        jnp.swapaxes(input_basis, 1, 2),
        jnp.swapaxes(output_basis, 1, 2),
        query_grads,
    )
    got = lax.all_to_all(send, ("ctx", "dp"), 0, 0)
    scores = pl.pallas_call(
        functools.partial(score_kernel, docs, rows, many, dp),
        out_shape=jax.ShapeDtypeStruct((peers, docs, peers * many), jnp.float32),
        in_specs=[smem, vmem],
        out_specs=vmem,
        compiler_params=pltpu.CompilerParams(vmem_limit_bytes=8 << 20),
        name="column_scores",
    )(doc_rank, got)
    got = lax.all_to_all(scores, ("ctx", "dp"), 0, 0)
    return jnp.sum(got, axis=0)


def solution(mesh):
    return jax.shard_map(
        functools.partial(local, dict(mesh.shape)),
        mesh=mesh,
        in_specs=(
            P(None, ("groups", "dp"), "ctx", None),
            P(None, ("groups", "dp"), "ctx", None),
            P(),
            P(),
            P(("groups", "ctx", "dp"), None),
            P(("groups", "dp")),
            P("groups"),
        ),
        out_specs=P(("groups", "dp"), None),
        check_vma=False,
    )
```

```python
import functools

import jax
import jax.numpy as jnp
from jax import lax
from jax.experimental import pallas as pl
from jax.experimental.pallas import tpu as pltpu
from jax.sharding import PartitionSpec as P

LANES = 128
BY_LAST = (((1,), (1,)), ((), ()))
BY_FIRST = (((0,), (0,)), ((), ()))


def partial_kernel(
    length_hbm, act_ref, outg_ref, inb_ref, outb_ref, query_hbm, send_ref,
    act_buf, outg_buf, inb, outb, query, rows_out, rows_in, square, flat, length_ref, act_sem, outg_sem, basis_sem, small_sem,
):
    layers, docs, tok, _ = act_ref.shape
    rank = inb_ref.shape[1]
    peers = send_ref.shape[0]
    per_layer = peers // layers
    rows = rank * rank // LANES // per_layer
    many = query.shape[0]
    first = lax.axis_index("ctx") * tok
    pairs = layers * docs

    def copies(pair):
        layer, doc = pair // docs, pair % docs
        return (
            pltpu.make_async_copy(outg_ref.at[layer, doc], outg_buf.at[pair], outg_sem.at[pair]),
            pltpu.make_async_copy(act_ref.at[layer, doc], act_buf.at[pair], act_sem.at[pair]),
        )

    def bases(layer):
        return (
            pltpu.make_async_copy(outb_ref.at[layer], outb.at[layer], basis_sem.at[layer, 0]),
            pltpu.make_async_copy(inb_ref.at[layer], inb.at[layer], basis_sem.at[layer, 1]),
        )

    def valid(pair):
        return first < length_ref[pair % docs]

    lengths = pltpu.make_async_copy(length_hbm, length_ref, small_sem.at[0])
    queries = pltpu.make_async_copy(query_hbm, query, small_sem.at[1])
    lengths.start()
    queries.start()
    for copy in bases(0):
        copy.start()
    lengths.wait()
    for pair in range(pairs):
        if pair > 0 and pair % docs == 0:
            for copy in bases(pair // docs):
                copy.start()

        @pl.when(valid(pair))
        def _(pair=pair):
            for copy in copies(pair):
                copy.start()

    queries.wait()
    for peer in range(peers):
        for row in range(rows):
            column = (peer * rows + row) * LANES
            at = docs * rows + row * many
            send_ref[peer, at : at + many, :] = query[:, column : column + LANES]

    def finish(pair):
        scale = lax.rsqrt(jnp.full((1, 1), length_ref[(pair + docs - 1) % docs], jnp.int32).astype(jnp.float32))
        other = (pair + 1) % 2
        square[...] = scale * lax.dot_general(
            rows_out[other], rows_in[other], BY_FIRST, preferred_element_type=jnp.float32
        )
        flat[pair] = jnp.concatenate(
            [square[pl.ds(0, rank // 2, stride=2), :], square[pl.ds(1, rank // 2, stride=2), :]], axis=1
        )

    def work(pair, _):
        layer, doc, slot = pair // docs, pair % docs, pair % 2

        @pl.when(doc == 0)
        def _():
            for copy in bases(layer):
                copy.wait()

        @pl.when(valid(pair))
        def _():
            for copy in copies(pair):
                copy.wait()
            out_rows = lax.dot_general(
                outg_buf[pair], outb[layer], BY_LAST, preferred_element_type=jnp.float32
            )
            in_rows = lax.dot_general(
                act_buf[pair], inb[layer], BY_LAST, preferred_element_type=jnp.float32
            )
            finish(pair)
            position = first + lax.broadcasted_iota(jnp.int32, out_rows.shape, 0)
            out_rows = jnp.where(position < length_ref[doc], out_rows, 0.0)
            rows_out[slot] = out_rows.astype(jnp.bfloat16)
            rows_in[slot] = in_rows.astype(jnp.bfloat16)

        @pl.when(jnp.logical_not(valid(pair)))
        def _():
            finish(pair)
            rows_out[slot] = jnp.zeros((tok, rank), jnp.bfloat16)
            rows_in[slot] = jnp.zeros((tok, rank), jnp.bfloat16)

        return 0

    rows_out[1] = jnp.zeros((tok, rank), jnp.bfloat16)
    rows_in[1] = jnp.zeros((tok, rank), jnp.bfloat16)
    lax.fori_loop(0, pairs, work, 0)
    finish(pairs)
    for layer in range(layers):
        for doc in range(docs):
            for j in range(per_layer):
                send_ref[layer * per_layer + j, doc * rows : (doc + 1) * rows, :] = flat[
                    layer * docs + doc + 1, j * rows : (j + 1) * rows
                ]


def score_kernel(docs, rows, many, dp, rank_ref, got_ref, send_ref):
    peers = got_ref.shape[0]
    total = dp * docs
    sums = []
    for d in range(dp):
        part = got_ref[d, : docs * rows, :]
        for c in range(1, peers // dp):
            part = part + got_ref[c * dp + d, : docs * rows, :]
        sums.append(part)
    score = jnp.zeros((total, peers * many), jnp.float32)
    for row in range(rows):
        grad = jnp.concatenate(
            [sums[d][k * rows + row : k * rows + row + 1] for d in range(dp) for k in range(docs)], axis=0
        )
        at = docs * rows + row * many
        query = got_ref[:, at : at + many, :].reshape(peers * many, LANES)
        score = score + lax.dot_general(
            grad, query, BY_LAST, precision=lax.Precision.HIGHEST, preferred_element_type=jnp.float32
        )
    placed = []
    for want in range(total):
        line = jnp.zeros((1, peers * many), jnp.float32)
        for k in range(total):
            line = jnp.where(rank_ref[k] == want, score[k : k + 1], line)
        placed.append(line)
    for d in range(dp):
        mine = jnp.concatenate(placed[d * docs : (d + 1) * docs], axis=0)
        for c in range(peers // dp):
            send_ref[c * dp + d] = mine


def local(mesh_shape, activations, out_grads, input_basis, output_basis, query_grads, doc_length, doc_rank):
    layers, docs, tok, width = activations.shape
    rank = input_basis.shape[2]
    many = query_grads.shape[0]
    dp = mesh_shape["dp"]
    peers = mesh_shape["ctx"] * dp
    rows = layers * rank * rank // LANES // peers
    pairs = layers * docs
    anywhere = pl.BlockSpec(memory_space=pl.ANY)
    vmem = pl.BlockSpec(memory_space=pltpu.VMEM)
    smem = pl.BlockSpec(memory_space=pltpu.SMEM)
    send = pl.pallas_call(
        partial_kernel,
        out_shape=jax.ShapeDtypeStruct((peers, (docs + many) * rows, LANES), jnp.float32),
        in_specs=[anywhere] * 6,
        out_specs=vmem,
        scratch_shapes=[
            pltpu.VMEM((pairs, tok, width), jnp.bfloat16),
            pltpu.VMEM((pairs, tok, width), jnp.bfloat16),
            pltpu.VMEM((layers, rank, width), jnp.bfloat16),
            pltpu.VMEM((layers, rank, width), jnp.bfloat16),
            pltpu.VMEM(query_grads.shape, jnp.float32),
            pltpu.VMEM((2, tok, rank), jnp.bfloat16),
            pltpu.VMEM((2, tok, rank), jnp.bfloat16),
            pltpu.VMEM((rank, rank), jnp.float32),
            pltpu.VMEM((pairs + 1, rank // 2, 2 * rank), jnp.float32),
            pltpu.SMEM((docs,), jnp.int32),
            pltpu.SemaphoreType.DMA((pairs,)),
            pltpu.SemaphoreType.DMA((pairs,)),
            pltpu.SemaphoreType.DMA((layers, 2)),
            pltpu.SemaphoreType.DMA((2,)),
        ],
        compiler_params=pltpu.CompilerParams(vmem_limit_bytes=60 << 20),
        name="partial_grads",
    )(
        doc_length,
        activations,
        out_grads,
        jnp.swapaxes(input_basis, 1, 2),
        jnp.swapaxes(output_basis, 1, 2),
        query_grads,
    )
    got = lax.all_to_all(send, ("ctx", "dp"), 0, 0)
    scores = pl.pallas_call(
        functools.partial(score_kernel, docs, rows, many, dp),
        out_shape=jax.ShapeDtypeStruct((peers, docs, peers * many), jnp.float32),
        in_specs=[smem, vmem],
        out_specs=vmem,
        compiler_params=pltpu.CompilerParams(vmem_limit_bytes=8 << 20),
        name="column_scores",
    )(doc_rank, got)
    got = lax.all_to_all(scores, ("ctx", "dp"), 0, 0)
    return jnp.sum(got, axis=0)


def solution(mesh):
    return jax.shard_map(
        functools.partial(local, dict(mesh.shape)),
        mesh=mesh,
        in_specs=(
            P(None, ("groups", "dp"), "ctx", None),
            P(None, ("groups", "dp"), "ctx", None),
            P(),
            P(),
            P(("groups", "ctx", "dp"), None),
            P(("groups", "dp")),
            P("groups"),
        ),
        out_specs=P(("groups", "dp"), None),
        check_vma=False,
    )
```

```python
import functools

import jax
import jax.numpy as jnp
from jax import lax
from jax.experimental import pallas as pl
from jax.experimental.pallas import tpu as pltpu
from jax.sharding import PartitionSpec as P

LANES = 128
BY_LAST = (((1,), (1,)), ((), ()))
BY_FIRST = (((0,), (0,)), ((), ()))


def partial_kernel(
    length_hbm, act_ref, outg_ref, inb_ref, outb_ref, query_hbm, send_hbm,
    act_buf, outg_buf, inb, outb, query, rows_out, rows_in, square, flat, send_ref, length_ref, act_sem, outg_sem, basis_sem, small_sem,
):
    layers, docs, tok, _ = act_ref.shape
    rank = inb_ref.shape[1]
    peers = send_ref.shape[0]
    per_layer = peers // layers
    rows = rank * rank // LANES // per_layer
    many = query.shape[0]
    first = lax.axis_index("ctx") * tok
    pairs = layers * docs

    def copies(pair):
        layer, doc = pair // docs, pair % docs
        return (
            pltpu.make_async_copy(outg_ref.at[layer, doc], outg_buf.at[pair], outg_sem.at[pair]),
            pltpu.make_async_copy(act_ref.at[layer, doc], act_buf.at[pair], act_sem.at[pair]),
        )

    def bases(layer):
        return (
            pltpu.make_async_copy(outb_ref.at[layer], outb.at[layer], basis_sem.at[layer, 0]),
            pltpu.make_async_copy(inb_ref.at[layer], inb.at[layer], basis_sem.at[layer, 1]),
        )

    def valid(pair):
        return first < length_ref[pair % docs]

    lengths = pltpu.make_async_copy(length_hbm, length_ref, small_sem.at[0])
    queries = pltpu.make_async_copy(query_hbm, query, small_sem.at[1])
    lengths.start()
    queries.start()
    for copy in bases(0):
        copy.start()
    lengths.wait()
    for pair in range(pairs):
        if pair > 0 and pair % docs == 0:
            for copy in bases(pair // docs):
                copy.start()

        @pl.when(valid(pair))
        def _(pair=pair):
            for copy in copies(pair):
                copy.start()

    queries.wait()
    for peer in range(peers):
        for row in range(rows):
            column = (peer * rows + row) * LANES
            at = docs * rows + row * many
            send_ref[peer, at : at + many, :] = query[:, column : column + LANES]

    late = docs * rows
    early = pltpu.make_async_copy(send_ref.at[:, late:], send_hbm.at[:, late:], small_sem.at[2])
    early.start()

    def finish(pair):
        scale = lax.rsqrt(jnp.full((1, 1), length_ref[(pair + docs - 1) % docs], jnp.int32).astype(jnp.float32))
        other = (pair + 1) % 2
        square[...] = scale * lax.dot_general(
            rows_out[other], rows_in[other], BY_FIRST, preferred_element_type=jnp.float32
        )
        flat[pair] = jnp.concatenate(
            [square[pl.ds(0, rank // 2, stride=2), :], square[pl.ds(1, rank // 2, stride=2), :]], axis=1
        )

    def work(pair, _):
        layer, doc, slot = pair // docs, pair % docs, pair % 2

        @pl.when(doc == 0)
        def _():
            for copy in bases(layer):
                copy.wait()

        @pl.when(valid(pair))
        def _():
            for copy in copies(pair):
                copy.wait()
            out_rows = lax.dot_general(
                outg_buf[pair], outb[layer], BY_LAST, preferred_element_type=jnp.float32
            )
            in_rows = lax.dot_general(
                act_buf[pair], inb[layer], BY_LAST, preferred_element_type=jnp.float32
            )
            finish(pair)
            position = first + lax.broadcasted_iota(jnp.int32, out_rows.shape, 0)
            out_rows = jnp.where(position < length_ref[doc], out_rows, 0.0)
            rows_out[slot] = out_rows.astype(jnp.bfloat16)
            rows_in[slot] = in_rows.astype(jnp.bfloat16)

        @pl.when(jnp.logical_not(valid(pair)))
        def _():
            finish(pair)
            rows_out[slot] = jnp.zeros((tok, rank), jnp.bfloat16)
            rows_in[slot] = jnp.zeros((tok, rank), jnp.bfloat16)

        return 0

    rows_out[1] = jnp.zeros((tok, rank), jnp.bfloat16)
    rows_in[1] = jnp.zeros((tok, rank), jnp.bfloat16)
    lax.fori_loop(0, pairs, work, 0)
    finish(pairs)
    for layer in range(layers):
        for doc in range(docs):
            for j in range(per_layer):
                send_ref[layer * per_layer + j, doc * rows : (doc + 1) * rows, :] = flat[
                    layer * docs + doc + 1, j * rows : (j + 1) * rows
                ]
    last = pltpu.make_async_copy(send_ref.at[:, :late], send_hbm.at[:, :late], small_sem.at[3])
    last.start()
    early.wait()
    last.wait()


def score_kernel(docs, rows, many, dp, rank_ref, got_ref, send_ref):
    peers = got_ref.shape[0]
    total = dp * docs
    sums = []
    for d in range(dp):
        part = got_ref[d, : docs * rows, :]
        for c in range(1, peers // dp):
            part = part + got_ref[c * dp + d, : docs * rows, :]
        sums.append(part)
    grad = jnp.concatenate(
        [
            jnp.concatenate([sums[d][k * rows + row : k * rows + row + 1] for row in range(rows)], axis=1)
            for d in range(dp)
            for k in range(docs)
        ],
        axis=0,
    )
    first = docs * rows
    query = jnp.concatenate(
        [
            got_ref[:, first + row * many : first + (row + 1) * many, :].reshape(peers * many, LANES)
            for row in range(rows)
        ],
        axis=1,
    )
    grad_high = grad.astype(jnp.bfloat16).astype(jnp.float32)
    query_high = query.astype(jnp.bfloat16)
    query_low = (query - query_high.astype(jnp.float32)).astype(jnp.bfloat16)
    both = jnp.concatenate([grad_high, grad - grad_high], axis=0).astype(jnp.bfloat16)
    by_high = lax.dot_general(both, query_high, BY_LAST, preferred_element_type=jnp.float32)
    by_low = lax.dot_general(both, query_low, BY_LAST, preferred_element_type=jnp.float32)
    score = by_high[:total] + (by_high[total:] + by_low[:total])
    placed = []
    for want in range(total):
        line = jnp.zeros((1, peers * many), jnp.float32)
        for k in range(total):
            line = jnp.where(rank_ref[k] == want, score[k : k + 1], line)
        placed.append(line)
    for d in range(dp):
        mine = jnp.concatenate(placed[d * docs : (d + 1) * docs], axis=0)
        for c in range(peers // dp):
            send_ref[c * dp + d] = mine


def local(mesh_shape, activations, out_grads, input_basis, output_basis, query_grads, doc_length, doc_rank):
    layers, docs, tok, width = activations.shape
    rank = input_basis.shape[2]
    many = query_grads.shape[0]
    dp = mesh_shape["dp"]
    peers = mesh_shape["ctx"] * dp
    rows = layers * rank * rank // LANES // peers
    pairs = layers * docs
    anywhere = pl.BlockSpec(memory_space=pl.ANY)
    vmem = pl.BlockSpec(memory_space=pltpu.VMEM)
    smem = pl.BlockSpec(memory_space=pltpu.SMEM)
    send = pl.pallas_call(
        partial_kernel,
        out_shape=jax.ShapeDtypeStruct((peers, (docs + many) * rows, LANES), jnp.float32),
        in_specs=[anywhere] * 6,
        out_specs=anywhere,
        scratch_shapes=[
            pltpu.VMEM((pairs, tok, width), jnp.bfloat16),
            pltpu.VMEM((pairs, tok, width), jnp.bfloat16),
            pltpu.VMEM((layers, rank, width), jnp.bfloat16),
            pltpu.VMEM((layers, rank, width), jnp.bfloat16),
            pltpu.VMEM(query_grads.shape, jnp.float32),
            pltpu.VMEM((2, tok, rank), jnp.bfloat16),
            pltpu.VMEM((2, tok, rank), jnp.bfloat16),
            pltpu.VMEM((rank, rank), jnp.float32),
            pltpu.VMEM((pairs + 1, rank // 2, 2 * rank), jnp.float32),
            pltpu.VMEM((peers, (docs + many) * rows, LANES), jnp.float32),
            pltpu.SMEM((docs,), jnp.int32),
            pltpu.SemaphoreType.DMA((pairs,)),
            pltpu.SemaphoreType.DMA((pairs,)),
            pltpu.SemaphoreType.DMA((layers, 2)),
            pltpu.SemaphoreType.DMA((4,)),
        ],
        compiler_params=pltpu.CompilerParams(vmem_limit_bytes=60 << 20),
        name="partial_grads",
    )(
        doc_length,
        activations,
        out_grads,
        jnp.swapaxes(input_basis, 1, 2),
        jnp.swapaxes(output_basis, 1, 2),
        query_grads,
    )
    got = lax.all_to_all(send, ("ctx", "dp"), 0, 0)
    scores = pl.pallas_call(
        functools.partial(score_kernel, docs, rows, many, dp),
        out_shape=jax.ShapeDtypeStruct((peers, docs, peers * many), jnp.float32),
        in_specs=[smem, vmem],
        out_specs=vmem,
        compiler_params=pltpu.CompilerParams(vmem_limit_bytes=8 << 20),
        name="column_scores",
    )(doc_rank, got)
    got = lax.all_to_all(scores, ("ctx", "dp"), 0, 0)
    return jnp.sum(got, axis=0)


def solution(mesh):
    return jax.shard_map(
        functools.partial(local, dict(mesh.shape)),
        mesh=mesh,
        in_specs=(
            P(None, ("groups", "dp"), "ctx", None),
            P(None, ("groups", "dp"), "ctx", None),
            P(),
            P(),
            P(("groups", "ctx", "dp"), None),
            P(("groups", "dp")),
            P("groups"),
        ),
        out_specs=P(("groups", "dp"), None),
        check_vma=False,
    )
```

```python
import functools

import jax
import jax.numpy as jnp
from jax import lax
from jax.experimental import pallas as pl
from jax.experimental.pallas import tpu as pltpu
from jax.sharding import PartitionSpec as P

LANES = 128
BY_LAST = (((1,), (1,)), ((), ()))
BY_FIRST = (((0,), (0,)), ((), ()))


def whole_tiles(rows):
    return -(-rows // 8) * 8


def partial_kernel(
    length_hbm, act_ref, outg_ref, inb_ref, outb_ref, query_hbm, send_hbm,
    act_buf, outg_buf, inb, outb, query, rows_out, rows_in, square, flat, send_ref, length_ref, act_sem, outg_sem, basis_sem, small_sem,
):
    layers, docs, tok, _ = act_ref.shape
    rank = inb_ref.shape[1]
    peers = send_ref.shape[0]
    per_layer = peers // layers
    rows = rank * rank // LANES // per_layer
    many = query.shape[0]
    head = whole_tiles(docs * rows)
    first = lax.axis_index("ctx") * tok
    pairs = layers * docs

    def copies(pair):
        layer, doc = pair // docs, pair % docs
        return (
            pltpu.make_async_copy(outg_ref.at[layer, doc], outg_buf.at[pair], outg_sem.at[pair]),
            pltpu.make_async_copy(act_ref.at[layer, doc], act_buf.at[pair], act_sem.at[pair]),
        )

    def bases(layer):
        return (
            pltpu.make_async_copy(outb_ref.at[layer], outb.at[layer], basis_sem.at[layer, 0]),
            pltpu.make_async_copy(inb_ref.at[layer], inb.at[layer], basis_sem.at[layer, 1]),
        )

    def valid(pair):
        return first < length_ref[pair % docs]

    lengths = pltpu.make_async_copy(length_hbm, length_ref, small_sem.at[0])
    queries = pltpu.make_async_copy(query_hbm, query, small_sem.at[1])
    lengths.start()
    queries.start()
    for copy in bases(0):
        copy.start()
    lengths.wait()
    for pair in range(pairs):
        if pair > 0 and pair % docs == 0:
            for copy in bases(pair // docs):
                copy.start()

        @pl.when(valid(pair))
        def _(pair=pair):
            for copy in copies(pair):
                copy.start()

    queries.wait()
    for peer in range(peers):
        for row in range(rows):
            column = (peer * rows + row) * LANES
            at = head + row * many
            send_ref[peer, at : at + many, :] = query[:, column : column + LANES]

    early = pltpu.make_async_copy(send_ref.at[:, head:], send_hbm.at[:, head:], small_sem.at[2])
    early.start()

    def finish(pair):
        scale = lax.rsqrt(jnp.full((1, 1), length_ref[(pair + docs - 1) % docs], jnp.int32).astype(jnp.float32))
        other = (pair + 1) % 2
        square[...] = scale * lax.dot_general(
            rows_out[other], rows_in[other], BY_FIRST, preferred_element_type=jnp.float32
        )
        flat[pair] = jnp.concatenate(
            [square[pl.ds(0, rank // 2, stride=2), :], square[pl.ds(1, rank // 2, stride=2), :]], axis=1
        )

    def work(pair, _):
        layer, doc, slot = pair // docs, pair % docs, pair % 2

        @pl.when(doc == 0)
        def _():
            for copy in bases(layer):
                copy.wait()

        @pl.when(valid(pair))
        def _():
            for copy in copies(pair):
                copy.wait()
            out_rows = lax.dot_general(
                outg_buf[pair], outb[layer], BY_LAST, preferred_element_type=jnp.float32
            )
            in_rows = lax.dot_general(
                act_buf[pair], inb[layer], BY_LAST, preferred_element_type=jnp.float32
            )
            finish(pair)
            position = first + lax.broadcasted_iota(jnp.int32, out_rows.shape, 0)
            out_rows = jnp.where(position < length_ref[doc], out_rows, 0.0)
            rows_out[slot] = out_rows.astype(jnp.bfloat16)
            rows_in[slot] = in_rows.astype(jnp.bfloat16)

        @pl.when(jnp.logical_not(valid(pair)))
        def _():
            finish(pair)
            rows_out[slot] = jnp.zeros((tok, rank), jnp.bfloat16)
            rows_in[slot] = jnp.zeros((tok, rank), jnp.bfloat16)

        return 0

    rows_out[1] = jnp.zeros((tok, rank), jnp.bfloat16)
    rows_in[1] = jnp.zeros((tok, rank), jnp.bfloat16)
    lax.fori_loop(0, pairs, work, 0)
    finish(pairs)
    for layer in range(layers):
        for doc in range(docs):
            for j in range(per_layer):
                send_ref[layer * per_layer + j, doc * rows : (doc + 1) * rows, :] = flat[
                    layer * docs + doc + 1, j * rows : (j + 1) * rows
                ]
    if head > docs * rows:
        send_ref[:, docs * rows : head, :] = jnp.zeros((peers, head - docs * rows, LANES), jnp.float32)
    last = pltpu.make_async_copy(send_ref.at[:, :head], send_hbm.at[:, :head], small_sem.at[3])
    last.start()
    early.wait()
    last.wait()


def score_kernel(docs, rows, many, dp, rank_ref, got_ref, send_ref):
    peers = got_ref.shape[0]
    total = dp * docs
    sums = []
    for d in range(dp):
        part = got_ref[d, : docs * rows, :]
        for c in range(1, peers // dp):
            part = part + got_ref[c * dp + d, : docs * rows, :]
        sums.append(part)
    grad = jnp.concatenate(
        [
            jnp.concatenate([sums[d][k * rows + row : k * rows + row + 1] for row in range(rows)], axis=1)
            for d in range(dp)
            for k in range(docs)
        ],
        axis=0,
    )
    first = whole_tiles(docs * rows)
    query = jnp.concatenate(
        [
            got_ref[:, first + row * many : first + (row + 1) * many, :].reshape(peers * many, LANES)
            for row in range(rows)
        ],
        axis=1,
    )
    grad_high = grad.astype(jnp.bfloat16).astype(jnp.float32)
    query_high = query.astype(jnp.bfloat16)
    query_low = (query - query_high.astype(jnp.float32)).astype(jnp.bfloat16)
    both = jnp.concatenate([grad_high, grad - grad_high], axis=0).astype(jnp.bfloat16)
    by_high = lax.dot_general(both, query_high, BY_LAST, preferred_element_type=jnp.float32)
    by_low = lax.dot_general(both, query_low, BY_LAST, preferred_element_type=jnp.float32)
    score = by_high[:total] + (by_high[total:] + by_low[:total])
    placed = []
    for want in range(total):
        line = jnp.zeros((1, peers * many), jnp.float32)
        for k in range(total):
            line = jnp.where(rank_ref[k] == want, score[k : k + 1], line)
        placed.append(line)
    for d in range(dp):
        mine = jnp.concatenate(placed[d * docs : (d + 1) * docs], axis=0)
        for c in range(peers // dp):
            send_ref[c * dp + d] = mine


def local(mesh_shape, activations, out_grads, input_basis, output_basis, query_grads, doc_length, doc_rank):
    layers, docs, tok, width = activations.shape
    rank = input_basis.shape[2]
    many = query_grads.shape[0]
    dp = mesh_shape["dp"]
    peers = mesh_shape["ctx"] * dp
    rows = layers * rank * rank // LANES // peers
    pairs = layers * docs
    sent = (peers, whole_tiles(docs * rows) + many * rows, LANES)
    anywhere = pl.BlockSpec(memory_space=pl.ANY)
    vmem = pl.BlockSpec(memory_space=pltpu.VMEM)
    smem = pl.BlockSpec(memory_space=pltpu.SMEM)
    send = pl.pallas_call(
        partial_kernel,
        out_shape=jax.ShapeDtypeStruct(sent, jnp.float32),
        in_specs=[anywhere] * 6,
        out_specs=anywhere,
        scratch_shapes=[
            pltpu.VMEM((pairs, tok, width), jnp.bfloat16),
            pltpu.VMEM((pairs, tok, width), jnp.bfloat16),
            pltpu.VMEM((layers, rank, width), jnp.bfloat16),
            pltpu.VMEM((layers, rank, width), jnp.bfloat16),
            pltpu.VMEM(query_grads.shape, jnp.float32),
            pltpu.VMEM((2, tok, rank), jnp.bfloat16),
            pltpu.VMEM((2, tok, rank), jnp.bfloat16),
            pltpu.VMEM((rank, rank), jnp.float32),
            pltpu.VMEM((pairs + 1, rank // 2, 2 * rank), jnp.float32),
            pltpu.VMEM(sent, jnp.float32),
            pltpu.SMEM((docs,), jnp.int32),
            pltpu.SemaphoreType.DMA((pairs,)),
            pltpu.SemaphoreType.DMA((pairs,)),
            pltpu.SemaphoreType.DMA((layers, 2)),
            pltpu.SemaphoreType.DMA((4,)),
        ],
        compiler_params=pltpu.CompilerParams(vmem_limit_bytes=60 << 20),
        name="partial_grads",
    )(
        doc_length,
        activations,
        out_grads,
        jnp.swapaxes(input_basis, 1, 2),
        jnp.swapaxes(output_basis, 1, 2),
        query_grads,
    )
    got = lax.all_to_all(send, ("ctx", "dp"), 0, 0)
    scores = pl.pallas_call(
        functools.partial(score_kernel, docs, rows, many, dp),
        out_shape=jax.ShapeDtypeStruct((peers, docs, peers * many), jnp.float32),
        in_specs=[smem, vmem],
        out_specs=vmem,
        compiler_params=pltpu.CompilerParams(vmem_limit_bytes=8 << 20),
        name="column_scores",
    )(doc_rank, got)
    got = lax.all_to_all(scores, ("ctx", "dp"), 0, 0)
    return jnp.sum(got, axis=0)


def solution(mesh):
    return jax.shard_map(
        functools.partial(local, dict(mesh.shape)),
        mesh=mesh,
        in_specs=(
            P(None, ("groups", "dp"), "ctx", None),
            P(None, ("groups", "dp"), "ctx", None),
            P(),
            P(),
            P(("groups", "ctx", "dp"), None),
            P(("groups", "dp")),
            P("groups"),
        ),
        out_specs=P(("groups", "dp"), None),
        check_vma=False,
    )
```

```python
import functools

import jax
import jax.numpy as jnp
from jax import lax
from jax.experimental import pallas as pl
from jax.experimental.pallas import tpu as pltpu
from jax.sharding import PartitionSpec as P

LANES = 128
BY_LAST = (((1,), (1,)), ((), ()))
BY_FIRST = (((0,), (0,)), ((), ()))


def whole_tiles(rows):
    return -(-rows // 8) * 8


def partial_kernel(
    length_hbm, act_ref, outg_ref, inb_ref, outb_ref, query_hbm, send_hbm,
    act_buf, outg_buf, inb, outb, query, rows_out, rows_in, square, flat, send_ref, length_ref, act_sem, outg_sem, basis_sem, small_sem,
):
    layers, docs, tok, _ = act_ref.shape
    rank = inb_ref.shape[1]
    peers = send_ref.shape[0]
    per_layer = peers // layers
    rows = rank * rank // LANES // per_layer
    many = query.shape[0]
    head = whole_tiles(docs * rows)
    first = lax.axis_index("ctx") * tok
    pairs = layers * docs

    def copies(pair):
        layer, doc = pair // docs, pair % docs
        return (
            pltpu.make_async_copy(outg_ref.at[layer, doc], outg_buf.at[pair], outg_sem.at[pair]),
            pltpu.make_async_copy(act_ref.at[layer, doc], act_buf.at[pair], act_sem.at[pair]),
        )

    bases = (
        pltpu.make_async_copy(outb_ref, outb, basis_sem.at[0]),
        pltpu.make_async_copy(inb_ref, inb, basis_sem.at[1]),
    )

    def valid(pair):
        return first < length_ref[pair % docs]

    lengths = pltpu.make_async_copy(length_hbm, length_ref, small_sem.at[0])
    queries = pltpu.make_async_copy(query_hbm, query, small_sem.at[1])
    lengths.start()
    queries.start()
    for copy in bases:
        copy.start()
    lengths.wait()
    for pair in range(pairs):

        @pl.when(valid(pair))
        def _(pair=pair):
            for copy in copies(pair):
                copy.start()

    queries.wait()
    for peer in range(peers):
        for row in range(rows):
            column = (peer * rows + row) * LANES
            at = head + row * many
            send_ref[peer, at : at + many, :] = query[:, column : column + LANES]

    early = pltpu.make_async_copy(send_ref.at[:, head:], send_hbm.at[:, head:], small_sem.at[2])
    early.start()

    def finish(pair):
        scale = lax.rsqrt(jnp.full((1, 1), length_ref[(pair + docs - 1) % docs], jnp.int32).astype(jnp.float32))
        other = (pair + 1) % 2
        square[...] = scale * lax.dot_general(
            rows_out[other], rows_in[other], BY_FIRST, preferred_element_type=jnp.float32
        )
        flat[pair] = jnp.concatenate(
            [square[pl.ds(0, rank // 2, stride=2), :], square[pl.ds(1, rank // 2, stride=2), :]], axis=1
        )

    def work(pair, _):
        layer, doc, slot = pair // docs, pair % docs, pair % 2

        @pl.when(valid(pair))
        def _():
            for copy in copies(pair):
                copy.wait()
            out_rows = lax.dot_general(
                outg_buf[pair], outb[layer], BY_LAST, preferred_element_type=jnp.float32
            )
            in_rows = lax.dot_general(
                act_buf[pair], inb[layer], BY_LAST, preferred_element_type=jnp.float32
            )
            finish(pair)
            position = first + lax.broadcasted_iota(jnp.int32, out_rows.shape, 0)
            out_rows = jnp.where(position < length_ref[doc], out_rows, 0.0)
            rows_out[slot] = out_rows.astype(jnp.bfloat16)
            rows_in[slot] = in_rows.astype(jnp.bfloat16)

        @pl.when(jnp.logical_not(valid(pair)))
        def _():
            finish(pair)
            rows_out[slot] = jnp.zeros((tok, rank), jnp.bfloat16)
            rows_in[slot] = jnp.zeros((tok, rank), jnp.bfloat16)

        return 0

    rows_out[1] = jnp.zeros((tok, rank), jnp.bfloat16)
    rows_in[1] = jnp.zeros((tok, rank), jnp.bfloat16)
    for copy in bases:
        copy.wait()
    lax.fori_loop(0, pairs, work, 0)
    finish(pairs)
    for layer in range(layers):
        for doc in range(docs):
            for j in range(per_layer):
                send_ref[layer * per_layer + j, doc * rows : (doc + 1) * rows, :] = flat[
                    layer * docs + doc + 1, j * rows : (j + 1) * rows
                ]
    if head > docs * rows:
        send_ref[:, docs * rows : head, :] = jnp.zeros((peers, head - docs * rows, LANES), jnp.float32)
    last = pltpu.make_async_copy(send_ref.at[:, :head], send_hbm.at[:, :head], small_sem.at[3])
    last.start()
    early.wait()
    last.wait()


def score_kernel(docs, rows, many, dp, rank_ref, got_ref, send_ref):
    peers = got_ref.shape[0]
    total = dp * docs
    sums = []
    for d in range(dp):
        part = got_ref[d, : docs * rows, :]
        for c in range(1, peers // dp):
            part = part + got_ref[c * dp + d, : docs * rows, :]
        sums.append(part)
    grad = jnp.concatenate(
        [
            jnp.concatenate([sums[d][k * rows + row : k * rows + row + 1] for row in range(rows)], axis=1)
            for d in range(dp)
            for k in range(docs)
        ],
        axis=0,
    )
    first = whole_tiles(docs * rows)
    query = jnp.concatenate(
        [
            got_ref[:, first + row * many : first + (row + 1) * many, :].reshape(peers * many, LANES)
            for row in range(rows)
        ],
        axis=1,
    )
    grad_high = grad.astype(jnp.bfloat16).astype(jnp.float32)
    query_high = query.astype(jnp.bfloat16)
    query_low = (query - query_high.astype(jnp.float32)).astype(jnp.bfloat16)
    both = jnp.concatenate([grad_high, grad - grad_high], axis=0).astype(jnp.bfloat16)
    by_high = lax.dot_general(both, query_high, BY_LAST, preferred_element_type=jnp.float32)
    by_low = lax.dot_general(both, query_low, BY_LAST, preferred_element_type=jnp.float32)
    score = by_high[:total] + (by_high[total:] + by_low[:total])
    placed = []
    for want in range(total):
        line = jnp.zeros((1, peers * many), jnp.float32)
        for k in range(total):
            line = jnp.where(rank_ref[k] == want, score[k : k + 1], line)
        placed.append(line)
    for d in range(dp):
        mine = jnp.concatenate(placed[d * docs : (d + 1) * docs], axis=0)
        for c in range(peers // dp):
            send_ref[c * dp + d] = mine


def local(mesh_shape, activations, out_grads, input_basis, output_basis, query_grads, doc_length, doc_rank):
    layers, docs, tok, width = activations.shape
    rank = input_basis.shape[2]
    many = query_grads.shape[0]
    dp = mesh_shape["dp"]
    peers = mesh_shape["ctx"] * dp
    rows = layers * rank * rank // LANES // peers
    pairs = layers * docs
    sent = (peers, whole_tiles(docs * rows) + many * rows, LANES)
    anywhere = pl.BlockSpec(memory_space=pl.ANY)
    vmem = pl.BlockSpec(memory_space=pltpu.VMEM)
    smem = pl.BlockSpec(memory_space=pltpu.SMEM)
    send = pl.pallas_call(
        partial_kernel,
        out_shape=jax.ShapeDtypeStruct(sent, jnp.float32),
        in_specs=[anywhere] * 6,
        out_specs=anywhere,
        scratch_shapes=[
            pltpu.VMEM((pairs, tok, width), jnp.bfloat16),
            pltpu.VMEM((pairs, tok, width), jnp.bfloat16),
            pltpu.VMEM((layers, rank, width), jnp.bfloat16),
            pltpu.VMEM((layers, rank, width), jnp.bfloat16),
            pltpu.VMEM(query_grads.shape, jnp.float32),
            pltpu.VMEM((2, tok, rank), jnp.bfloat16),
            pltpu.VMEM((2, tok, rank), jnp.bfloat16),
            pltpu.VMEM((rank, rank), jnp.float32),
            pltpu.VMEM((pairs + 1, rank // 2, 2 * rank), jnp.float32),
            pltpu.VMEM(sent, jnp.float32),
            pltpu.SMEM((docs,), jnp.int32),
            pltpu.SemaphoreType.DMA((pairs,)),
            pltpu.SemaphoreType.DMA((pairs,)),
            pltpu.SemaphoreType.DMA((2,)),
            pltpu.SemaphoreType.DMA((4,)),
        ],
        compiler_params=pltpu.CompilerParams(vmem_limit_bytes=60 << 20),
        name="partial_grads",
    )(
        doc_length,
        activations,
        out_grads,
        jnp.swapaxes(input_basis, 1, 2),
        jnp.swapaxes(output_basis, 1, 2),
        query_grads,
    )
    got = lax.all_to_all(send, ("ctx", "dp"), 0, 0)
    scores = pl.pallas_call(
        functools.partial(score_kernel, docs, rows, many, dp),
        out_shape=jax.ShapeDtypeStruct((peers, docs, peers * many), jnp.float32),
        in_specs=[smem, vmem],
        out_specs=vmem,
        compiler_params=pltpu.CompilerParams(vmem_limit_bytes=8 << 20),
        name="column_scores",
    )(doc_rank, got)
    got = lax.all_to_all(scores, ("ctx", "dp"), 0, 0)
    return jnp.sum(got, axis=0)


def solution(mesh):
    return jax.shard_map(
        functools.partial(local, dict(mesh.shape)),
        mesh=mesh,
        in_specs=(
            P(None, ("groups", "dp"), "ctx", None),
            P(None, ("groups", "dp"), "ctx", None),
            P(),
            P(),
            P(("groups", "ctx", "dp"), None),
            P(("groups", "dp")),
            P("groups"),
        ),
        out_specs=P(("groups", "dp"), None),
        check_vma=False,
    )
```
